32 devices in a mesh: sec: 8 (over z, x), fld: 4 (over y, core).
Axes of the slice: x: 2, y: 2, z: 4, core: 2. Of those that a mesh axis runs over, the one named last changes fastest.
Arguments:
- surface: float32 [4, 256, 512], P('fld', 'sec'), may hold values from -6 to 6
- diffusivity: float32 [4, 256, 512], P('fld', 'sec'), may hold values from 0.02 to 0.24
- send_list: int32 [8, 8, 171], P('sec'), may hold values from 0 to 127
- recv_slot: int32 [1024, 4], P('sec'), may hold values from 0 to 1367, as said below
- weights: bfloat16 [1024, 4, 128, 128], P(('sec', 'fld')), may hold values from -0.25 to 0.25
Outputs:
- stepped: float32 [4, 256, 512], P('fld', 'sec')
- remapped: float32 [4, 256, 512], P('fld', 'sec')
The draws below stay inside these ranges and needn't reach their ends.
Inputs may be any that keep to these rules, and one draw needn't show every extreme that they name: `recv_slot`: the 512 entries of one device's target blocks are distinct slots, all of devices of the other component; from one source device to one target device at most 171 slots are used, and that many in some pair.
All inputs are finite; a program needn't handle non-finite values.
Results may differ from the reference program's by a relative error of at most 0.0029.
Values may be sent and summed in bfloat16 or wider, within the bound.
A program may use at most 64 MiB of HBM per device.

```python
import math
import jax
import jax.numpy as jnp
from jax import lax

ROWS = 32
COLS = 512
SUBSTEPS = 4
K = 4
FIELDS = 4
BLK = 128
N_ATMD = 3
CAP = 171
GROWS = 256
TBLK = 1024
N_SEC = 8


def draw_recv_slot(key, part):
    slots = N_SEC * CAP
    positions = jnp.arange(slots, dtype=jnp.int32)
    slot_ocean = positions // CAP >= N_ATMD

    def one_target(target):
        own_ocean = target >= N_ATMD
        rank = jax.random.permutation(jax.random.fold_in(key, target), slots).astype(jnp.int32)
        same = (slot_ocean == own_ocean).astype(jnp.int32)
        score = same * slots + rank
        forced = jnp.where(own_ocean, positions == 0, positions == slots - 1)
        score = jnp.where(forced, -1, score)
        order = jnp.argsort(score)[:BLK * K].astype(jnp.int32)
        mixing = jax.random.permutation(jax.random.fold_in(key, target + 7919), BLK * K)
        return order[mixing].reshape(BLK, K)
    table = jax.vmap(one_target)(jnp.arange(N_SEC, dtype=jnp.int32))
    return table.reshape(N_SEC * BLK, K).astype(jnp.int32)


def place_ends(drawn, key, smallest, largest):
    longest = drawn.shape.index(max(drawn.shape))
    spots = []
    for shift in (0, 1):
        where = [jax.random.randint(jax.random.fold_in(key, axis), (), 0, length) for axis, length in enumerate(drawn.shape)]
        where[longest] = (where[longest] + shift) % drawn.shape[longest]
        spots.append(tuple(where))
    return drawn.at[spots[0]].set(smallest).at[spots[1]].set(largest)


def steps_of(key, dims, shards, smallest, high):
    loudness, own = 1.0, jax.random.fold_in(key, 6)
    for axis_at, blocks in shards:
        draws = jnp.exp(jax.random.uniform(jax.random.fold_in(own, axis_at), (blocks,), jnp.float32, smallest / len(shards), high / len(shards)))
        loudness = loudness * jnp.repeat(draws, dims[axis_at] // blocks).reshape([-1 if axis == axis_at else 1 for axis in range(len(dims))])
    return loudness


def bell_draw(stream_key, shape, width, bound, cuts=(), kind=jnp.bfloat16):
    drawn = jax.random.normal(stream_key, shape, jnp.float32) * width
    if len(cuts) > 0:
        drawn = steps_of(stream_key, shape, cuts, -0.22, 0.18) * drawn
    return jnp.clip(drawn, min=-bound, max=bound).astype(kind)


def setup_inputs(seed: int = 0) -> dict:
    keys = jax.random.split(jax.random.key(seed), 6)
    surface = bell_draw(keys[0], (FIELDS, GROWS, COLS), 1.0, 6.0, ((0, 4), (1, 8)), jnp.float32)
    diffusivity = jnp.clip(jnp.exp(math.log(0.24) - 2.4849066 * jax.random.uniform(keys[1], (FIELDS, GROWS, COLS), jnp.float32) ** steps_of(keys[1], (FIELDS, GROWS, COLS), ((0, 4), (1, 8)), -0.2, 0.2)), 0.02, 0.24)
    send_list = place_ends(jax.random.randint(keys[2], (N_SEC, N_SEC, CAP), 0, BLK), jax.random.fold_in(keys[2], 1), 0, BLK - 1).astype(jnp.int32)
    recv_slot = draw_recv_slot(jax.random.fold_in(keys[5], 71), 0)
    weights = bell_draw(keys[4], (TBLK, K, 128, 128), (K * 128) ** -0.5, 0.25, ((0, 32),))
    return {"surface": surface, "diffusivity": diffusivity, "send_list": send_list, "recv_slot": recv_slot, "weights": weights}


def diffuse(field, kappa):
    for step in range(SUBSTEPS):
        padded = jnp.pad(field, ((0, 0), (1, 1), (0, 0)))
        upper = padded[:, :-2]
        lower = padded[:, 2:]
        lap = upper + lower + jnp.roll(field, 1, 2) + jnp.roll(field, -1, 2) - 4.0 * field
        field = field + kappa * lap
    return field


def reference(surface, diffusivity, send_list, recv_slot, weights):
    split_row = N_ATMD * ROWS
    atmos = diffuse(surface[:, :split_row], diffusivity[:, :split_row])
    ocean = diffuse(surface[:, split_row:], diffusivity[:, split_row:])
    stepped = jnp.concatenate([atmos, ocean], 1)
    blocks = stepped.reshape(FIELDS, TBLK, 128).astype(jnp.bfloat16)
    target_dev = (jnp.arange(TBLK, dtype=jnp.int32) // BLK)[:, None]
    src_dev = recv_slot // CAP
    src_block = src_dev * BLK + send_list[src_dev, target_dev, recv_slot % CAP]
    source = blocks[:, src_block.reshape(-1)].reshape(FIELDS, N_SEC, BLK, K, 128)
    source = jnp.moveaxis(source, 1, 0)
    wparts = weights.reshape(N_SEC, BLK, K, 128, 128)

    def remap_one(pair):
        wpart, spart = pair
        return jnp.einsum("tkij,ftkj->fti", wpart.astype(jnp.float32), spart.astype(jnp.float32))

    outs = lax.map(remap_one, (wparts, source))
    remapped = jnp.moveaxis(outs, 0, 1).reshape(FIELDS, GROWS, COLS)
    return stepped, remapped
```

```python
import functools

import jax
import jax.numpy as jnp
from jax import lax
from jax.experimental import pallas as pl
from jax.experimental.pallas import tpu as pltpu
from jax.sharding import PartitionSpec as P

SUBSTEPS = 4
EDGE = 8
MESH = pl.DeviceIdType.MESH
F32 = jnp.float32
BF16 = jnp.bfloat16


def diffuse(u, kappa):
    rows, cols = u.shape
    for _ in range(SUBSTEPS):
        around = (
            pltpu.roll(u, 1, 0)
            + pltpu.roll(u, rows - 1, 0)
            + pltpu.roll(u, 1, 1)
            + pltpu.roll(u, cols - 1, 1)
        )
        u = u + kappa * (around - 4.0 * u)
    return u


def columns_of(x, width):
    return jnp.concatenate(
        [x[:, c : c + width] for c in range(0, x.shape[1], width)], axis=0
    )


def block_ids(shape, rows, per_row):
    inner = rows - EDGE
    p = lax.broadcasted_iota(jnp.int32, shape, 0)
    ids = jnp.zeros(shape, jnp.int32)
    for c in range(per_row):
        start = c * inner
        row = p - start + SUBSTEPS
        ids = jnp.where((p >= start) & (p < start + inner), row * per_row + c, ids)
        start = per_row * inner + c * EDGE
        row = p - start
        row = jnp.where(row < SUBSTEPS, row, row + inner)
        ids = jnp.where((p >= start) & (p < start + EDGE), row * per_row + c, ids)
    return ids


def kernel(
    n_sec, n_fld, surf, kap, sl, rst, w_hbm, stepped, remapped,
    halo, wv, sl_in, blk, land, cmat, acc, gbf, gath, xs, ys, ret, back, res,
    w_sem, halo_send, halo_recv, sl_send, sl_recv, in_send, in_recv,
    ed_send, ed_recv, g_send, g_recv, r_send, r_recv,
):
    rows, cols = surf.shape[1], surf.shape[2]
    width = wv.shape[3]
    per_row = cols // width
    n_blk = rows * per_row
    n_inner = (rows - EDGE) * per_row
    cap = sl.shape[2]
    n_k, n_t = rst.shape
    t_loc = n_t // n_fld

    me_s = lax.axis_index("sec")
    me_f = lax.axis_index("fld")
    atmos = n_sec * 3 // 8
    is_ocean = me_s >= atmos
    own_base = jnp.where(is_ocean, atmos, 0)
    own_end = jnp.where(is_ocean, n_sec, atmos)
    oth_base = jnp.where(is_ocean, 0, atmos)
    n_oth = jnp.where(is_ocean, atmos, n_sec - atmos)
    has_up = me_s > own_base
    has_dn = me_s < own_end - 1
    mine = me_s - own_base

    w_copy = pltpu.make_async_copy(w_hbm, wv, w_sem)
    w_copy.start()

    barrier = pltpu.get_barrier_semaphore()

    @pl.when(has_up)
    def _():
        pl.semaphore_signal(barrier, 1, device_id={"sec": me_s - 1, "fld": me_f}, device_id_type=MESH)

    @pl.when(has_dn)
    def _():
        pl.semaphore_signal(barrier, 1, device_id={"sec": me_s + 1, "fld": me_f}, device_id_type=MESH)

    @pl.loop(0, n_oth)
    def _(j):
        pl.semaphore_signal(barrier, 1, device_id={"sec": oth_base + j, "fld": me_f}, device_id_type=MESH)

    for i in range(1, n_fld):
        pl.semaphore_signal(
            barrier, 1, device_id={"sec": me_s, "fld": lax.rem(me_f + i, n_fld)}, device_id_type=MESH
        )

    inner = diffuse(surf[0], kap[0])[SUBSTEPS : rows - SUBSTEPS]
    stepped[0, SUBSTEPS : rows - SUBSTEPS, :] = inner
    blk[0:n_inner, :] = columns_of(inner, width).astype(BF16)

    pl.semaphore_wait(
        barrier, n_oth + has_up.astype(jnp.int32) + has_dn.astype(jnp.int32) + (n_fld - 1)
    )

    def halo_copy(which, side):
        ref = (surf, kap)[which]
        first, to = ((rows - EDGE, me_s + 1), (0, me_s - 1))[side]
        return pltpu.make_async_remote_copy(
            src_ref=ref.at[0, pl.ds(first, EDGE), :],
            dst_ref=halo.at[which, side],
            send_sem=halo_send.at[which, side],
            recv_sem=halo_recv.at[which, side],
            device_id={"sec": to, "fld": me_f},
            device_id_type=MESH,
        )

    @pl.when(has_dn)
    def _():
        halo_copy(0, 0).start()
        halo_copy(1, 0).start()

    @pl.when(has_up)
    def _():
        halo_copy(0, 1).start()
        halo_copy(1, 1).start()

    def sl_copy(j, slot):
        target = oth_base + j
        return pltpu.make_async_remote_copy(
            src_ref=sl.at[0, pl.ds(pl.multiple_of(target // 8 * 8, 8), 8), :],
            dst_ref=sl_in.at[slot],
            send_sem=sl_send.at[j],
            recv_sem=sl_recv.at[slot],
            device_id={"sec": target, "fld": me_f},
            device_id_type=MESH,
        )

    def block_copy(j, slot, edge):
        part = pl.ds(n_inner, n_blk - n_inner) if edge else pl.ds(0, n_inner)
        return pltpu.make_async_remote_copy(
            src_ref=blk.at[part],
            dst_ref=land.at[slot, part],
            send_sem=(ed_send if edge else in_send).at[j],
            recv_sem=(ed_recv if edge else in_recv).at[slot],
            device_id={"sec": oth_base + j, "fld": me_f},
            device_id_type=MESH,
        )

    @pl.loop(0, n_oth)
    def _(j):
        sl_copy(j, mine).start()

    @pl.loop(0, n_oth)
    def _(j):
        block_copy(j, mine, False).start()

    @pl.when(has_up)
    def _():
        halo_copy(0, 0).wait_recv()
        halo_copy(1, 0).wait_recv()

    @pl.when(jnp.logical_not(has_up))
    def _():
        halo[:, 0] = jnp.zeros((2, EDGE, cols), F32)

    @pl.when(has_dn)
    def _():
        halo_copy(0, 1).wait_recv()
        halo_copy(1, 1).wait_recv()

    @pl.when(jnp.logical_not(has_dn))
    def _():
        halo[:, 1] = jnp.zeros((2, EDGE, cols), F32)

    def around_edges(which):
        ref = (surf, kap)[which]
        return jnp.concatenate(
            [halo[which, 0], ref[0, 0:EDGE, :], ref[0, rows - EDGE : rows, :], halo[which, 1]], axis=0
        )

    edges = diffuse(around_edges(0), around_edges(1))
    top, bottom = edges[EDGE : 2 * EDGE], edges[2 * EDGE : 3 * EDGE]
    upper = lax.broadcasted_iota(jnp.int32, (EDGE, cols), 0) < SUBSTEPS
    edge = jnp.where(upper, top, bottom)
    stepped[0, 0:SUBSTEPS, :] = edge[0:SUBSTEPS]
    stepped[0, rows - SUBSTEPS : rows, :] = edge[SUBSTEPS:EDGE]
    blk[n_inner:n_blk, :] = columns_of(edge, width).astype(BF16)

    @pl.loop(0, n_oth)
    def _(j):
        block_copy(j, mine, True).start()

    ids = block_ids((n_blk, cap), rows, per_row)
    slot_of = lax.broadcasted_iota(jnp.int32, (cap, n_t), 0)

    @pl.loop(0, n_oth)
    def _(j):
        sl_copy(j, j).wait_recv()
        sent = sl_in[j, pl.ds(lax.rem(me_s, 8), 1), :]
        pick = jnp.where(ids == sent, 1.0, 0.0).astype(BF16)
        slots = slot_of + (oth_base + j) * cap
        for k in range(n_k):
            put = jnp.where(rst[k : k + 1, :] == slots, 1.0, 0.0).astype(BF16)
            chosen = jnp.dot(pick, put, preferred_element_type=F32)
            cmat[j, k * n_t : (k + 1) * n_t, :] = chosen.T.astype(BF16)

    acc[...] = jnp.zeros_like(acc)

    @pl.loop(0, n_oth)
    def _(j):
        block_copy(j, j, False).wait_recv()
        block_copy(j, j, True).wait_recv()
        acc[...] += jnp.dot(cmat[j], land[j], preferred_element_type=F32)

    for k in range(n_k):
        gbf[k] = acc[k * n_t : (k + 1) * n_t, :].astype(BF16)

    def pair_copy(i, slot):
        to = lax.rem(me_f + i, n_fld)
        return pltpu.make_async_remote_copy(
            src_ref=gbf.at[:, pl.ds(pl.multiple_of(to * t_loc, t_loc), t_loc), :],
            dst_ref=gath.at[slot],
            send_sem=g_send.at[i],
            recv_sem=g_recv.at[i],
            device_id={"sec": me_s, "fld": to},
            device_id_type=MESH,
        )

    for i in range(1, n_fld):
        pair_copy(i, me_f).start()
    gath[me_f] = gbf[:, pl.ds(pl.multiple_of(me_f * t_loc, t_loc), t_loc), :]
    w_copy.wait()
    for i in range(1, n_fld):
        pair_copy(i, lax.rem(me_f + n_fld - i, n_fld)).wait_recv()

    for f in range(n_fld):
        for k in range(n_k):
            xs[k, pl.ds(f, t_loc, stride=n_fld), :] = gath[f, k].astype(F32)

    group = 8 // n_fld
    which_t = lax.broadcasted_iota(jnp.int32, (8, width), 0) // n_fld

    def remap(g, carry):
        at = pl.multiple_of(g * 8, 8)
        x = jnp.concatenate([xs[k, pl.ds(at, 8), :] for k in range(n_k)], axis=1).astype(BF16)
        y = jnp.zeros((8, width), F32)
        for u in range(group):
            w = jnp.concatenate([wv[g * group + u, k] for k in range(n_k)], axis=1)
            full = lax.dot_general(x, w, (((1,), (1,)), ((), ())), preferred_element_type=F32)
            y = jnp.where(which_t == u, full, y)
        ys[pl.ds(at, 8), :] = y
        return carry

    lax.fori_loop(0, t_loc // group, remap, 0, unroll=4)

    for f in range(n_fld):
        ret[f] = ys[pl.ds(f, t_loc, stride=n_fld), :].astype(BF16)

    def return_copy(i, slot):
        to = lax.rem(me_f + i, n_fld)
        return pltpu.make_async_remote_copy(
            src_ref=ret.at[to],
            dst_ref=back.at[slot],
            send_sem=r_send.at[i],
            recv_sem=r_recv.at[i],
            device_id={"sec": me_s, "fld": to},
            device_id_type=MESH,
        )

    for i in range(1, n_fld):
        return_copy(i, me_f).start()
    back[me_f] = ret[me_f]
    for i in range(1, n_fld):
        return_copy(i, lax.rem(me_f + n_fld - i, n_fld)).wait_recv()
    for q in range(n_fld):
        res[q * t_loc : (q + 1) * t_loc, :] = back[q].astype(F32)
    for c in range(per_row):
        remapped[0, :, c * width : (c + 1) * width] = res[pl.ds(c, rows, stride=per_row), :]

    @pl.when(has_dn)
    def _():
        halo_copy(0, 0).wait_send()
        halo_copy(1, 0).wait_send()

    @pl.when(has_up)
    def _():
        halo_copy(0, 1).wait_send()
        halo_copy(1, 1).wait_send()

    @pl.loop(0, n_oth)
    def _(j):
        sl_copy(j, mine).wait_send()
        block_copy(j, mine, False).wait_send()
        block_copy(j, mine, True).wait_send()

    for i in range(1, n_fld):
        pair_copy(i, me_f).wait_send()
        return_copy(i, me_f).wait_send()


def per_device(n_sec, n_fld, surface, diffusivity, send_list, recv_slot, weights):
    _, rows, cols = surface.shape
    t_loc, n_k, width, _ = weights.shape
    n_t = recv_slot.shape[0]
    n_blk = rows * cols // width
    cap = send_list.shape[2]
    most = n_sec - n_sec * 3 // 8
    vmem = pl.BlockSpec(memory_space=pltpu.VMEM)
    dma = pltpu.SemaphoreType.DMA
    shape = jax.ShapeDtypeStruct(surface.shape, F32)
    return pl.pallas_call(
        functools.partial(kernel, n_sec, n_fld),
        out_shape=(shape, shape),
        in_specs=[vmem, vmem, vmem, vmem, pl.BlockSpec(memory_space=pl.ANY)],
        out_specs=(vmem, vmem),
        scratch_shapes=[
            pltpu.VMEM((2, 2, EDGE, cols), F32),
            pltpu.VMEM(weights.shape, BF16),
            pltpu.VMEM((most, 8, cap), jnp.int32),
            pltpu.VMEM((n_blk, width), BF16),
            pltpu.VMEM((most, n_blk, width), BF16),
            pltpu.VMEM((most, n_k * n_t, n_blk), BF16),
            pltpu.VMEM((n_k * n_t, width), F32),
            pltpu.VMEM((n_k, n_t, width), BF16),
            pltpu.VMEM((n_fld, n_k, t_loc, width), BF16),
            pltpu.VMEM((n_k, t_loc * n_fld, width), F32),
            pltpu.VMEM((t_loc * n_fld, width), F32),
            pltpu.VMEM((n_fld, t_loc, width), BF16),
            pltpu.VMEM((n_fld, t_loc, width), BF16),
            pltpu.VMEM((n_blk, width), F32),
            dma,
            dma((2, 2)),
            dma((2, 2)),
            dma((most,)),
            dma((most,)),
            dma((most,)),
            dma((most,)),
            dma((most,)),
            dma((most,)),
            dma((n_fld,)),
            dma((n_fld,)),
            dma((n_fld,)),
            dma((n_fld,)),
        ],
        compiler_params=pltpu.CompilerParams(
            collective_id=0, has_side_effects=True, vmem_limit_bytes=48 * 1024 * 1024
        ),
    )(surface, diffusivity, send_list, recv_slot.T, weights)


def solution(mesh):
    return jax.shard_map(
        functools.partial(per_device, mesh.shape["sec"], mesh.shape["fld"]),
        mesh=mesh,
        in_specs=(
            P("fld", "sec", None),
            P("fld", "sec", None),
            P("sec", None, None),
            P("sec", None),
            P(("sec", "fld"), None, None, None),
        ),
        out_specs=(P("fld", "sec", None), P("fld", "sec", None)),
        check_vma=False,
    )
```

```python
import functools

import jax
import jax.numpy as jnp
from jax import lax
from jax.experimental import pallas as pl
from jax.experimental.pallas import tpu as pltpu
from jax.sharding import PartitionSpec as P

SUBSTEPS = 4
EDGE = 8
MESH = pl.DeviceIdType.MESH
F32 = jnp.float32
BF16 = jnp.bfloat16


def diffuse(u, kappa):
    rows, cols = u.shape
    for _ in range(SUBSTEPS):
        around = (
            pltpu.roll(u, 1, 0)
            + pltpu.roll(u, rows - 1, 0)
            + pltpu.roll(u, 1, 1)
            + pltpu.roll(u, cols - 1, 1)
        )
        u = u + kappa * (around - 4.0 * u)
    return u


def columns_of(x, width):
    return jnp.concatenate(
        [x[:, c : c + width] for c in range(0, x.shape[1], width)], axis=0
    )


def block_ids(shape, rows, per_row):
    inner = rows - EDGE
    p = lax.broadcasted_iota(jnp.int32, shape, 0)
    ids = jnp.zeros(shape, jnp.int32)
    for c in range(per_row):
        start = c * inner
        row = p - start + SUBSTEPS
        ids = jnp.where((p >= start) & (p < start + inner), row * per_row + c, ids)
        start = per_row * inner + c * EDGE
        row = p - start
        row = jnp.where(row < SUBSTEPS, row, row + inner)
        ids = jnp.where((p >= start) & (p < start + EDGE), row * per_row + c, ids)
    return ids


def kernel(
    n_sec, n_fld, surf_hbm, kap_hbm, sl_hbm, rst_hbm, w_hbm, stepped, remapped,
    surf, kap, sl, rst, halo, wv, sl_in, blk, land, cmat, acc, gbf, gath, xs, ys, ret, back, res,
    load_sem, halo_send, halo_recv, sl_send, sl_recv, in_send, in_recv,
    ed_send, ed_recv, g_send, g_recv, r_send, r_recv,
):
    rows, cols = surf.shape[1], surf.shape[2]
    width = wv.shape[3]
    per_row = cols // width
    n_blk = rows * per_row
    n_inner = (rows - EDGE) * per_row
    cap = sl.shape[2]
    n_k, n_t = rst.shape
    t_loc = n_t // n_fld

    me_s = lax.axis_index("sec")
    me_f = lax.axis_index("fld")
    atmos = n_sec * 3 // 8
    is_ocean = me_s >= atmos
    own_base = jnp.where(is_ocean, atmos, 0)
    own_end = jnp.where(is_ocean, n_sec, atmos)
    oth_base = jnp.where(is_ocean, 0, atmos)
    n_oth = jnp.where(is_ocean, atmos, n_sec - atmos)
    has_up = me_s > own_base
    has_dn = me_s < own_end - 1
    mine = me_s - own_base

    loads = [
        pltpu.make_async_copy(src, dst, load_sem.at[i])
        for i, (src, dst) in enumerate(
            ((surf_hbm, surf), (kap_hbm, kap), (sl_hbm, sl), (rst_hbm, rst), (w_hbm, wv))
        )
    ]
    for load in loads:
        load.start()

    barrier = pltpu.get_barrier_semaphore()

    @pl.when(has_up)
    def _():
        pl.semaphore_signal(barrier, 1, device_id={"sec": me_s - 1, "fld": me_f}, device_id_type=MESH)

    @pl.when(has_dn)
    def _():
        pl.semaphore_signal(barrier, 1, device_id={"sec": me_s + 1, "fld": me_f}, device_id_type=MESH)

    @pl.loop(0, n_oth)
    def _(j):
        pl.semaphore_signal(barrier, 1, device_id={"sec": oth_base + j, "fld": me_f}, device_id_type=MESH)

    for i in range(1, n_fld):
        pl.semaphore_signal(
            barrier, 1, device_id={"sec": me_s, "fld": lax.rem(me_f + i, n_fld)}, device_id_type=MESH
        )

    loads[0].wait()
    loads[1].wait()
    inner = diffuse(surf[0], kap[0])[SUBSTEPS : rows - SUBSTEPS]
    stepped[0, SUBSTEPS : rows - SUBSTEPS, :] = inner
    blk[0:n_inner, :] = columns_of(inner, width).astype(BF16)

    loads[2].wait()
    loads[3].wait()
    pl.semaphore_wait(
        barrier, n_oth + has_up.astype(jnp.int32) + has_dn.astype(jnp.int32) + (n_fld - 1)
    )

    def halo_copy(which, side):
        ref = (surf, kap)[which]
        first, to = ((rows - EDGE, me_s + 1), (0, me_s - 1))[side]
        return pltpu.make_async_remote_copy(
            src_ref=ref.at[0, pl.ds(first, EDGE), :],
            dst_ref=halo.at[which, side],
            send_sem=halo_send.at[which, side],
            recv_sem=halo_recv.at[which, side],
            device_id={"sec": to, "fld": me_f},
            device_id_type=MESH,
        )

    @pl.when(has_dn)
    def _():
        halo_copy(0, 0).start()
        halo_copy(1, 0).start()

    @pl.when(has_up)
    def _():
        halo_copy(0, 1).start()
        halo_copy(1, 1).start()

    def sl_copy(j, slot):
        target = oth_base + j
        return pltpu.make_async_remote_copy(
            src_ref=sl.at[0, pl.ds(pl.multiple_of(target // 8 * 8, 8), 8), :],
            dst_ref=sl_in.at[slot],
            send_sem=sl_send.at[j],
            recv_sem=sl_recv.at[slot],
            device_id={"sec": target, "fld": me_f},
            device_id_type=MESH,
        )

    def block_copy(j, slot, edge):
        part = pl.ds(n_inner, n_blk - n_inner) if edge else pl.ds(0, n_inner)
        return pltpu.make_async_remote_copy(
            src_ref=blk.at[part],
            dst_ref=land.at[slot, part],
            send_sem=(ed_send if edge else in_send).at[j],
            recv_sem=(ed_recv if edge else in_recv).at[slot],
            device_id={"sec": oth_base + j, "fld": me_f},
            device_id_type=MESH,
        )

    @pl.loop(0, n_oth)
    def _(j):
        sl_copy(j, mine).start()

    @pl.loop(0, n_oth)
    def _(j):
        block_copy(j, mine, False).start()

    @pl.when(has_up)
    def _():
        halo_copy(0, 0).wait_recv()
        halo_copy(1, 0).wait_recv()

    @pl.when(jnp.logical_not(has_up))
    def _():
        halo[:, 0] = jnp.zeros((2, EDGE, cols), F32)

    @pl.when(has_dn)
    def _():
        halo_copy(0, 1).wait_recv()
        halo_copy(1, 1).wait_recv()

    @pl.when(jnp.logical_not(has_dn))
    def _():
        halo[:, 1] = jnp.zeros((2, EDGE, cols), F32)

    def around_edges(which):
        ref = (surf, kap)[which]
        return jnp.concatenate(
            [halo[which, 0], ref[0, 0:EDGE, :], ref[0, rows - EDGE : rows, :], halo[which, 1]], axis=0
        )

    edges = diffuse(around_edges(0), around_edges(1))
    top, bottom = edges[EDGE : 2 * EDGE], edges[2 * EDGE : 3 * EDGE]
    upper = lax.broadcasted_iota(jnp.int32, (EDGE, cols), 0) < SUBSTEPS
    edge = jnp.where(upper, top, bottom)
    stepped[0, 0:SUBSTEPS, :] = edge[0:SUBSTEPS]
    stepped[0, rows - SUBSTEPS : rows, :] = edge[SUBSTEPS:EDGE]
    blk[n_inner:n_blk, :] = columns_of(edge, width).astype(BF16)

    @pl.loop(0, n_oth)
    def _(j):
        block_copy(j, mine, True).start()

    ids = block_ids((n_blk, cap), rows, per_row)
    slot_of = lax.broadcasted_iota(jnp.int32, (cap, n_t), 0)

    @pl.loop(0, n_oth)
    def _(j):
        sl_copy(j, j).wait_recv()
        sent = sl_in[j, pl.ds(lax.rem(me_s, 8), 1), :]
        pick = jnp.where(ids == sent, 1.0, 0.0).astype(BF16)
        slots = slot_of + (oth_base + j) * cap
        for k in range(n_k):
            put = jnp.where(rst[k : k + 1, :] == slots, 1.0, 0.0).astype(BF16)
            chosen = jnp.dot(pick, put, preferred_element_type=F32)
            cmat[j, k * n_t : (k + 1) * n_t, :] = chosen.T.astype(BF16)

    acc[...] = jnp.zeros_like(acc)

    @pl.loop(0, n_oth)
    def _(j):
        block_copy(j, j, False).wait_recv()
        block_copy(j, j, True).wait_recv()
        acc[...] += jnp.dot(cmat[j], land[j], preferred_element_type=F32)

    for k in range(n_k):
        gbf[k] = acc[k * n_t : (k + 1) * n_t, :].astype(BF16)

    def pair_copy(i, slot):
        to = lax.rem(me_f + i, n_fld)
        return pltpu.make_async_remote_copy(
            src_ref=gbf.at[:, pl.ds(pl.multiple_of(to * t_loc, t_loc), t_loc), :],
            dst_ref=gath.at[slot],
            send_sem=g_send.at[i],
            recv_sem=g_recv.at[i],
            device_id={"sec": me_s, "fld": to},
            device_id_type=MESH,
        )

    for i in range(1, n_fld):
        pair_copy(i, me_f).start()
    gath[me_f] = gbf[:, pl.ds(pl.multiple_of(me_f * t_loc, t_loc), t_loc), :]
    loads[4].wait()
    for i in range(1, n_fld):
        pair_copy(i, lax.rem(me_f + n_fld - i, n_fld)).wait_recv()

    for f in range(n_fld):
        for k in range(n_k):
            xs[k, pl.ds(f, t_loc, stride=n_fld), :] = gath[f, k].astype(F32)

    group = 8 // n_fld
    which_t = lax.broadcasted_iota(jnp.int32, (8, width), 0) // n_fld

    def remap(g, carry):
        at = pl.multiple_of(g * 8, 8)
        x = jnp.concatenate([xs[k, pl.ds(at, 8), :] for k in range(n_k)], axis=1).astype(BF16)
        y = jnp.zeros((8, width), F32)
        for u in range(group):
            w = jnp.concatenate([wv[g * group + u, k] for k in range(n_k)], axis=1)
            full = lax.dot_general(x, w, (((1,), (1,)), ((), ())), preferred_element_type=F32)
            y = jnp.where(which_t == u, full, y)
        ys[pl.ds(at, 8), :] = y
        return carry

    lax.fori_loop(0, t_loc // group, remap, 0, unroll=4)

    for f in range(n_fld):
        ret[f] = ys[pl.ds(f, t_loc, stride=n_fld), :].astype(BF16)

    def return_copy(i, slot):
        to = lax.rem(me_f + i, n_fld)
        return pltpu.make_async_remote_copy(
            src_ref=ret.at[to],
            dst_ref=back.at[slot],
            send_sem=r_send.at[i],
            recv_sem=r_recv.at[i],
            device_id={"sec": me_s, "fld": to},
            device_id_type=MESH,
        )

    for i in range(1, n_fld):
        return_copy(i, me_f).start()
    back[me_f] = ret[me_f]
    for i in range(1, n_fld):
        return_copy(i, lax.rem(me_f + n_fld - i, n_fld)).wait_recv()
    for q in range(n_fld):
        res[q * t_loc : (q + 1) * t_loc, :] = back[q].astype(F32)
    for c in range(per_row):
        remapped[0, :, c * width : (c + 1) * width] = res[pl.ds(c, rows, stride=per_row), :]

    @pl.when(has_dn)
    def _():
        halo_copy(0, 0).wait_send()
        halo_copy(1, 0).wait_send()

    @pl.when(has_up)
    def _():
        halo_copy(0, 1).wait_send()
        halo_copy(1, 1).wait_send()

    @pl.loop(0, n_oth)
    def _(j):
        sl_copy(j, mine).wait_send()
        block_copy(j, mine, False).wait_send()
        block_copy(j, mine, True).wait_send()

    for i in range(1, n_fld):
        pair_copy(i, me_f).wait_send()
        return_copy(i, me_f).wait_send()


def per_device(n_sec, n_fld, surface, diffusivity, send_list, recv_slot, weights):
    _, rows, cols = surface.shape
    t_loc, n_k, width, _ = weights.shape
    n_t = recv_slot.shape[0]
    n_blk = rows * cols // width
    cap = send_list.shape[2]
    most = n_sec - n_sec * 3 // 8
    vmem = pl.BlockSpec(memory_space=pltpu.VMEM)
    dma = pltpu.SemaphoreType.DMA
    shape = jax.ShapeDtypeStruct(surface.shape, F32)
    return pl.pallas_call(
        functools.partial(kernel, n_sec, n_fld),
        out_shape=(shape, shape),
        in_specs=[pl.BlockSpec(memory_space=pltpu.HBM)] * 5,
        out_specs=(vmem, vmem),
        scratch_shapes=[
            pltpu.VMEM(surface.shape, F32),
            pltpu.VMEM(surface.shape, F32),
            pltpu.VMEM(send_list.shape, jnp.int32),
            pltpu.VMEM((n_k, n_t), jnp.int32),
            pltpu.VMEM((2, 2, EDGE, cols), F32),
            pltpu.VMEM(weights.shape, BF16),
            pltpu.VMEM((most, 8, cap), jnp.int32),
            pltpu.VMEM((n_blk, width), BF16),
            pltpu.VMEM((most, n_blk, width), BF16),
            pltpu.VMEM((most, n_k * n_t, n_blk), BF16),
            pltpu.VMEM((n_k * n_t, width), F32),
            pltpu.VMEM((n_k, n_t, width), BF16),
            pltpu.VMEM((n_fld, n_k, t_loc, width), BF16),
            pltpu.VMEM((n_k, t_loc * n_fld, width), F32),
            pltpu.VMEM((t_loc * n_fld, width), F32),
            pltpu.VMEM((n_fld, t_loc, width), BF16),
            pltpu.VMEM((n_fld, t_loc, width), BF16),
            pltpu.VMEM((n_blk, width), F32),
            dma((5,)),
            dma((2, 2)),
            dma((2, 2)),
            dma((most,)),
            dma((most,)),
            dma((most,)),
            dma((most,)),
            dma((most,)),
            dma((most,)),
            dma((n_fld,)),
            dma((n_fld,)),
            dma((n_fld,)),
            dma((n_fld,)),
        ],
        compiler_params=pltpu.CompilerParams(
            collective_id=0, has_side_effects=True, vmem_limit_bytes=63 * 1024 * 1024
        ),
    )(surface, diffusivity, send_list, recv_slot.T, weights)


def solution(mesh):
    return jax.shard_map(
        functools.partial(per_device, mesh.shape["sec"], mesh.shape["fld"]),
        mesh=mesh,
        in_specs=(
            P("fld", "sec", None),
            P("fld", "sec", None),
            P("sec", None, None),
            P("sec", None),
            P(("sec", "fld"), None, None, None),
        ),
        out_specs=(P("fld", "sec", None), P("fld", "sec", None)),
        check_vma=False,
    )
```

```python
import functools

import jax
import jax.numpy as jnp
from jax import lax
from jax.experimental import pallas as pl
from jax.experimental.pallas import tpu as pltpu
from jax.sharding import PartitionSpec as P

SUBSTEPS = 4
EDGE = 8
MESH = pl.DeviceIdType.MESH
F32 = jnp.float32
BF16 = jnp.bfloat16


def diffuse(u, kappa):
    rows, cols = u.shape
    for _ in range(SUBSTEPS):
        around = (
            pltpu.roll(u, 1, 0)
            + pltpu.roll(u, rows - 1, 0)
            + pltpu.roll(u, 1, 1)
            + pltpu.roll(u, cols - 1, 1)
        )
        u = u + kappa * (around - 4.0 * u)
    return u


def columns_of(x, width):
    return jnp.concatenate(
        [x[:, c : c + width] for c in range(0, x.shape[1], width)], axis=0
    )


def block_ids(shape, rows, per_row):
    inner = rows - EDGE
    p = lax.broadcasted_iota(jnp.int32, shape, 0)
    ids = jnp.zeros(shape, jnp.int32)
    for c in range(per_row):
        start = c * inner
        row = p - start + SUBSTEPS
        ids = jnp.where((p >= start) & (p < start + inner), row * per_row + c, ids)
        start = per_row * inner + c * EDGE
        row = p - start
        row = jnp.where(row < SUBSTEPS, row, row + inner)
        ids = jnp.where((p >= start) & (p < start + EDGE), row * per_row + c, ids)
    return ids


def kernel(
    n_sec, n_fld, surf_hbm, kap_hbm, sl_hbm, rst_hbm, w_hbm, out,
    surf, kap, sl, rst, halo, wv, sl_in, blk, land, cmat, acc, gbf, gath, xs, ys, ret, back, res,
    load_sem, halo_send, halo_recv, sl_send, sl_recv, in_send, in_recv,
    ed_send, ed_recv, g_send, g_recv, r_send, r_recv,
):
    rows, cols = surf.shape[1], surf.shape[2]
    width = wv.shape[3]
    per_row = cols // width
    n_blk = rows * per_row
    n_inner = (rows - EDGE) * per_row
    cap = sl.shape[2]
    n_k, n_t = rst.shape
    t_loc = n_t // n_fld

    me_s = lax.axis_index("sec")
    me_f = lax.axis_index("fld")
    atmos = n_sec * 3 // 8
    is_ocean = me_s >= atmos
    own_base = jnp.where(is_ocean, atmos, 0)
    own_end = jnp.where(is_ocean, n_sec, atmos)
    oth_base = jnp.where(is_ocean, 0, atmos)
    n_oth = jnp.where(is_ocean, atmos, n_sec - atmos)
    has_up = me_s > own_base
    has_dn = me_s < own_end - 1
    mine = me_s - own_base

    loads = [
        pltpu.make_async_copy(src, dst, load_sem.at[i])
        for i, (src, dst) in enumerate(
            ((surf_hbm, surf), (kap_hbm, kap), (sl_hbm, sl), (rst_hbm, rst), (w_hbm, wv))
        )
    ]
    for load in loads:
        load.start()

    barrier = pltpu.get_barrier_semaphore()

    @pl.when(has_up)
    def _():
        pl.semaphore_signal(barrier, 1, device_id={"sec": me_s - 1, "fld": me_f}, device_id_type=MESH)

    @pl.when(has_dn)
    def _():
        pl.semaphore_signal(barrier, 1, device_id={"sec": me_s + 1, "fld": me_f}, device_id_type=MESH)

    @pl.loop(0, n_oth)
    def _(j):
        pl.semaphore_signal(barrier, 1, device_id={"sec": oth_base + j, "fld": me_f}, device_id_type=MESH)

    for i in range(1, n_fld):
        pl.semaphore_signal(
            barrier, 1, device_id={"sec": me_s, "fld": lax.rem(me_f + i, n_fld)}, device_id_type=MESH
        )

    loads[0].wait()
    loads[1].wait()
    inner = diffuse(surf[0], kap[0])[SUBSTEPS : rows - SUBSTEPS]
    out[0, SUBSTEPS : rows - SUBSTEPS, :] = inner
    blk[0:n_inner, :] = columns_of(inner, width).astype(BF16)

    loads[2].wait()
    loads[3].wait()
    pl.semaphore_wait(
        barrier, n_oth + has_up.astype(jnp.int32) + has_dn.astype(jnp.int32) + (n_fld - 1)
    )

    def halo_copy(which, side):
        ref = (surf, kap)[which]
        first, to = ((rows - EDGE, me_s + 1), (0, me_s - 1))[side]
        return pltpu.make_async_remote_copy(
            src_ref=ref.at[0, pl.ds(first, EDGE), :],
            dst_ref=halo.at[which, side],
            send_sem=halo_send.at[which, side],
            recv_sem=halo_recv.at[which, side],
            device_id={"sec": to, "fld": me_f},
            device_id_type=MESH,
        )

    @pl.when(has_dn)
    def _():
        halo_copy(0, 0).start()
        halo_copy(1, 0).start()

    @pl.when(has_up)
    def _():
        halo_copy(0, 1).start()
        halo_copy(1, 1).start()

    def sl_copy(j, slot):
        target = oth_base + j
        return pltpu.make_async_remote_copy(
            src_ref=sl.at[0, pl.ds(pl.multiple_of(target // 8 * 8, 8), 8), :],
            dst_ref=sl_in.at[slot],
            send_sem=sl_send.at[j],
            recv_sem=sl_recv.at[slot],
            device_id={"sec": target, "fld": me_f},
            device_id_type=MESH,
        )

    def block_copy(j, slot, edge):
        part = pl.ds(n_inner, n_blk - n_inner) if edge else pl.ds(0, n_inner)
        return pltpu.make_async_remote_copy(
            src_ref=blk.at[part],
            dst_ref=land.at[slot, part],
            send_sem=(ed_send if edge else in_send).at[j],
            recv_sem=(ed_recv if edge else in_recv).at[slot],
            device_id={"sec": oth_base + j, "fld": me_f},
            device_id_type=MESH,
        )

    @pl.loop(0, n_oth)
    def _(j):
        sl_copy(j, mine).start()

    @pl.loop(0, n_oth)
    def _(j):
        block_copy(j, mine, False).start()

    @pl.when(has_up)
    def _():
        halo_copy(0, 0).wait_recv()
        halo_copy(1, 0).wait_recv()

    @pl.when(jnp.logical_not(has_up))
    def _():
        halo[:, 0] = jnp.zeros((2, EDGE, cols), F32)

    @pl.when(has_dn)
    def _():
        halo_copy(0, 1).wait_recv()
        halo_copy(1, 1).wait_recv()

    @pl.when(jnp.logical_not(has_dn))
    def _():
        halo[:, 1] = jnp.zeros((2, EDGE, cols), F32)

    def around_edges(which):
        ref = (surf, kap)[which]
        return jnp.concatenate(
            [halo[which, 0], ref[0, 0:EDGE, :], ref[0, rows - EDGE : rows, :], halo[which, 1]], axis=0
        )

    edges = diffuse(around_edges(0), around_edges(1))
    top, bottom = edges[EDGE : 2 * EDGE], edges[2 * EDGE : 3 * EDGE]
    upper = lax.broadcasted_iota(jnp.int32, (EDGE, cols), 0) < SUBSTEPS
    edge = jnp.where(upper, top, bottom)
    out[0, 0:SUBSTEPS, :] = edge[0:SUBSTEPS]
    out[0, rows - SUBSTEPS : rows, :] = edge[SUBSTEPS:EDGE]
    blk[n_inner:n_blk, :] = columns_of(edge, width).astype(BF16)

    @pl.loop(0, n_oth)
    def _(j):
        block_copy(j, mine, True).start()

    ids = block_ids((n_blk, cap), rows, per_row)
    slot_of = lax.broadcasted_iota(jnp.int32, (cap, n_t), 0)

    @pl.loop(0, n_oth)
    def _(j):
        sl_copy(j, j).wait_recv()
        sent = sl_in[j, pl.ds(lax.rem(me_s, 8), 1), :]
        pick = jnp.where(ids == sent, 1.0, 0.0).astype(BF16)
        slots = slot_of + (oth_base + j) * cap
        for k in range(n_k):
            put = jnp.where(rst[k : k + 1, :] == slots, 1.0, 0.0).astype(BF16)
            chosen = jnp.dot(pick, put, preferred_element_type=F32)
            cmat[j, k * n_t : (k + 1) * n_t, :] = chosen.T.astype(BF16)

    acc[...] = jnp.zeros_like(acc)

    @pl.loop(0, n_oth)
    def _(j):
        block_copy(j, j, False).wait_recv()
        block_copy(j, j, True).wait_recv()
        acc[...] += jnp.dot(cmat[j], land[j], preferred_element_type=F32)

    for k in range(n_k):
        gbf[k] = acc[k * n_t : (k + 1) * n_t, :].astype(BF16)

    def pair_copy(i, slot):
        to = lax.rem(me_f + i, n_fld)
        return pltpu.make_async_remote_copy(
            src_ref=gbf.at[:, pl.ds(pl.multiple_of(to * t_loc, t_loc), t_loc), :],
            dst_ref=gath.at[slot],
            send_sem=g_send.at[i],
            recv_sem=g_recv.at[i],
            device_id={"sec": me_s, "fld": to},
            device_id_type=MESH,
        )

    for i in range(1, n_fld):
        pair_copy(i, me_f).start()
    gath[me_f] = gbf[:, pl.ds(pl.multiple_of(me_f * t_loc, t_loc), t_loc), :]
    loads[4].wait()
    for i in range(1, n_fld):
        pair_copy(i, lax.rem(me_f + n_fld - i, n_fld)).wait_recv()

    for f in range(n_fld):
        for k in range(n_k):
            xs[k, pl.ds(f, t_loc, stride=n_fld), :] = gath[f, k].astype(F32)

    group = 8 // n_fld
    which_t = lax.broadcasted_iota(jnp.int32, (8, width), 0) // n_fld

    def remap(g, carry):
        at = pl.multiple_of(g * 8, 8)
        x = jnp.concatenate([xs[k, pl.ds(at, 8), :] for k in range(n_k)], axis=1).astype(BF16)
        y = jnp.zeros((8, width), F32)
        for u in range(group):
            w = jnp.concatenate([wv[g * group + u, k] for k in range(n_k)], axis=1)
            full = lax.dot_general(x, w, (((1,), (1,)), ((), ())), preferred_element_type=F32)
            y = jnp.where(which_t == u, full, y)
        ys[pl.ds(at, 8), :] = y
        return carry

    lax.fori_loop(0, t_loc // group, remap, 0, unroll=4)

    for f in range(n_fld):
        ret[f] = ys[pl.ds(f, t_loc, stride=n_fld), :].astype(BF16)

    def return_copy(i, slot):
        to = lax.rem(me_f + i, n_fld)
        return pltpu.make_async_remote_copy(
            src_ref=ret.at[to],
            dst_ref=back.at[slot],
            send_sem=r_send.at[i],
            recv_sem=r_recv.at[i],
            device_id={"sec": me_s, "fld": to},
            device_id_type=MESH,
        )

    for i in range(1, n_fld):
        return_copy(i, me_f).start()
    back[me_f] = ret[me_f]
    for i in range(1, n_fld):
        return_copy(i, lax.rem(me_f + n_fld - i, n_fld)).wait_recv()
    for q in range(n_fld):
        res[q * t_loc : (q + 1) * t_loc, :] = back[q].astype(F32)
    for c in range(per_row):
        out[1, :, c * width : (c + 1) * width] = res[pl.ds(c, rows, stride=per_row), :]

    @pl.when(has_dn)
    def _():
        halo_copy(0, 0).wait_send()
        halo_copy(1, 0).wait_send()

    @pl.when(has_up)
    def _():
        halo_copy(0, 1).wait_send()
        halo_copy(1, 1).wait_send()

    @pl.loop(0, n_oth)
    def _(j):
        sl_copy(j, mine).wait_send()
        block_copy(j, mine, False).wait_send()
        block_copy(j, mine, True).wait_send()

    for i in range(1, n_fld):
        pair_copy(i, me_f).wait_send()
        return_copy(i, me_f).wait_send()


def per_device(n_sec, n_fld, surface, diffusivity, send_list, recv_slot, weights):
    _, rows, cols = surface.shape
    t_loc, n_k, width, _ = weights.shape
    n_t = recv_slot.shape[0]
    n_blk = rows * cols // width
    cap = send_list.shape[2]
    most = n_sec - n_sec * 3 // 8
    vmem = pl.BlockSpec(memory_space=pltpu.VMEM)
    dma = pltpu.SemaphoreType.DMA
    operands = [pltpu.with_memory_space_constraint(x, pltpu.HBM) for x in (surface, diffusivity, send_list, recv_slot.T, weights)]
    both = pl.pallas_call(
        functools.partial(kernel, n_sec, n_fld),
        out_shape=pltpu.VMEM((2, rows, cols), F32),
        in_specs=[pl.BlockSpec(memory_space=pltpu.HBM)] * 5,
        out_specs=vmem,
        scratch_shapes=[
            pltpu.VMEM(surface.shape, F32),
            pltpu.VMEM(surface.shape, F32),
            pltpu.VMEM(send_list.shape, jnp.int32),
            pltpu.VMEM((n_k, n_t), jnp.int32),
            pltpu.VMEM((2, 2, EDGE, cols), F32),
            pltpu.VMEM(weights.shape, BF16),
            pltpu.VMEM((most, 8, cap), jnp.int32),
            pltpu.VMEM((n_blk, width), BF16),
            pltpu.VMEM((most, n_blk, width), BF16),
            pltpu.VMEM((most, n_k * n_t, n_blk), BF16),
            pltpu.VMEM((n_k * n_t, width), F32),
            pltpu.VMEM((n_k, n_t, width), BF16),
            pltpu.VMEM((n_fld, n_k, t_loc, width), BF16),
            pltpu.VMEM((n_k, t_loc * n_fld, width), F32),
            pltpu.VMEM((t_loc * n_fld, width), F32),
            pltpu.VMEM((n_fld, t_loc, width), BF16),
            pltpu.VMEM((n_fld, t_loc, width), BF16),
            pltpu.VMEM((n_blk, width), F32),
            dma((5,)),
            dma((2, 2)),
            dma((2, 2)),
            dma((most,)),
            dma((most,)),
            dma((most,)),
            dma((most,)),
            dma((most,)),
            dma((most,)),
            dma((n_fld,)),
            dma((n_fld,)),
            dma((n_fld,)),
            dma((n_fld,)),
        ],
        compiler_params=pltpu.CompilerParams(
            collective_id=0, has_side_effects=True, vmem_limit_bytes=48 * 1024 * 1024
        ),
    )(*operands)
    return both[0:1], both[1:2]


def solution(mesh):
    return jax.shard_map(
        functools.partial(per_device, mesh.shape["sec"], mesh.shape["fld"]),
        mesh=mesh,
        in_specs=(
            P("fld", "sec", None),
            P("fld", "sec", None),
            P("sec", None, None),
            P("sec", None),
            P(("sec", "fld"), None, None, None),
        ),
        out_specs=(P("fld", "sec", None), P("fld", "sec", None)),
        check_vma=False,
    )
```

```python
import functools

import jax
import jax.numpy as jnp
from jax import lax
from jax.experimental import pallas as pl
from jax.experimental.pallas import tpu as pltpu
from jax.sharding import PartitionSpec as P

SUBSTEPS = 4
EDGE = 8
MESH = pl.DeviceIdType.MESH
F32 = jnp.float32
BF16 = jnp.bfloat16


def diffuse(u, kappa):
    rows, cols = u.shape
    for _ in range(SUBSTEPS):
        around = (
            pltpu.roll(u, 1, 0)
            + pltpu.roll(u, rows - 1, 0)
            + pltpu.roll(u, 1, 1)
            + pltpu.roll(u, cols - 1, 1)
        )
        u = u + kappa * (around - 4.0 * u)
    return u


def columns_of(x, width):
    return jnp.concatenate(
        [x[:, c : c + width] for c in range(0, x.shape[1], width)], axis=0
    )


def block_ids(shape, rows, per_row):
    inner = rows - EDGE
    p = lax.broadcasted_iota(jnp.int32, shape, 0)
    ids = jnp.zeros(shape, jnp.int32)
    for c in range(per_row):
        start = c * inner
        row = p - start + SUBSTEPS
        ids = jnp.where((p >= start) & (p < start + inner), row * per_row + c, ids)
        start = per_row * inner + c * EDGE
        row = p - start
        row = jnp.where(row < SUBSTEPS, row, row + inner)
        ids = jnp.where((p >= start) & (p < start + EDGE), row * per_row + c, ids)
    return ids


def kernel(
    n_sec, n_fld, surf_hbm, kap_hbm, sl_hbm, rst_hbm, w_hbm, out,
    surf, kap, sl, rst, halo, wv, sl_in, blk, land, cmat, asked, acc, gbf, gath, xs, ys, ret, back, res,
    load_sem, halo_send, halo_recv, sl_send, sl_recv, in_send, in_recv,
    ed_send, ed_recv, g_send, g_recv, r_send, r_recv,
):
    rows, cols = surf.shape[1], surf.shape[2]
    width = wv.shape[3]
    per_row = cols // width
    n_blk = rows * per_row
    n_inner = (rows - EDGE) * per_row
    cap = sl.shape[2]
    n_k, n_t = rst.shape
    t_loc = n_t // n_fld

    me_s = lax.axis_index("sec")
    me_f = lax.axis_index("fld")
    atmos = n_sec * 3 // 8
    is_ocean = me_s >= atmos
    own_base = jnp.where(is_ocean, atmos, 0)
    own_end = jnp.where(is_ocean, n_sec, atmos)
    oth_base = jnp.where(is_ocean, 0, atmos)
    n_oth = jnp.where(is_ocean, atmos, n_sec - atmos)
    has_up = me_s > own_base
    has_dn = me_s < own_end - 1
    mine = me_s - own_base

    loads = [
        pltpu.make_async_copy(src, dst, load_sem.at[i])
        for i, (src, dst) in enumerate(
            ((surf_hbm, surf), (kap_hbm, kap), (sl_hbm, sl), (rst_hbm, rst), (w_hbm, wv))
        )
    ]
    for load in loads:
        load.start()

    barrier = pltpu.get_barrier_semaphore()

    @pl.when(has_up)
    def _():
        pl.semaphore_signal(barrier, 1, device_id={"sec": me_s - 1, "fld": me_f}, device_id_type=MESH)

    @pl.when(has_dn)
    def _():
        pl.semaphore_signal(barrier, 1, device_id={"sec": me_s + 1, "fld": me_f}, device_id_type=MESH)

    @pl.loop(0, n_oth)
    def _(j):
        pl.semaphore_signal(barrier, 1, device_id={"sec": oth_base + j, "fld": me_f}, device_id_type=MESH)

    for i in range(1, n_fld):
        pl.semaphore_signal(
            barrier, 1, device_id={"sec": me_s, "fld": lax.rem(me_f + i, n_fld)}, device_id_type=MESH
        )

    loads[0].wait()
    loads[1].wait()
    inner = diffuse(surf[0], kap[0])[SUBSTEPS : rows - SUBSTEPS]
    out[0, SUBSTEPS : rows - SUBSTEPS, :] = inner
    blk[0:n_inner, :] = columns_of(inner, width).astype(BF16)

    loads[2].wait()
    loads[3].wait()
    for k in range(n_k):
        row = jnp.broadcast_to(rst[k : k + 1, :].astype(F32), (width, n_t))
        asked[k * n_t : (k + 1) * n_t, :] = row.T

    pl.semaphore_wait(
        barrier, n_oth + has_up.astype(jnp.int32) + has_dn.astype(jnp.int32) + (n_fld - 1)
    )

    def halo_copy(which, side):
        ref = (surf, kap)[which]
        first, to = ((rows - EDGE, me_s + 1), (0, me_s - 1))[side]
        return pltpu.make_async_remote_copy(
            src_ref=ref.at[0, pl.ds(first, EDGE), :],
            dst_ref=halo.at[which, side],
            send_sem=halo_send.at[which, side],
            recv_sem=halo_recv.at[which, side],
            device_id={"sec": to, "fld": me_f},
            device_id_type=MESH,
        )

    @pl.when(has_dn)
    def _():
        halo_copy(0, 0).start()
        halo_copy(1, 0).start()

    @pl.when(has_up)
    def _():
        halo_copy(0, 1).start()
        halo_copy(1, 1).start()

    def sl_copy(j, slot):
        target = oth_base + j
        return pltpu.make_async_remote_copy(
            src_ref=sl.at[0, pl.ds(pl.multiple_of(target // 8 * 8, 8), 8), :],
            dst_ref=sl_in.at[slot],
            send_sem=sl_send.at[j],
            recv_sem=sl_recv.at[slot],
            device_id={"sec": target, "fld": me_f},
            device_id_type=MESH,
        )

    def block_copy(j, slot, edge):
        part = pl.ds(n_inner, n_blk - n_inner) if edge else pl.ds(0, n_inner)
        return pltpu.make_async_remote_copy(
            src_ref=blk.at[part],
            dst_ref=land.at[slot, part],
            send_sem=(ed_send if edge else in_send).at[j],
            recv_sem=(ed_recv if edge else in_recv).at[slot],
            device_id={"sec": oth_base + j, "fld": me_f},
            device_id_type=MESH,
        )

    @pl.loop(0, n_oth)
    def _(j):
        sl_copy(j, mine).start()

    @pl.loop(0, n_oth)
    def _(j):
        block_copy(j, mine, False).start()

    @pl.when(has_up)
    def _():
        halo_copy(0, 0).wait_recv()
        halo_copy(1, 0).wait_recv()

    @pl.when(jnp.logical_not(has_up))
    def _():
        halo[:, 0] = jnp.zeros((2, EDGE, cols), F32)

    @pl.when(has_dn)
    def _():
        halo_copy(0, 1).wait_recv()
        halo_copy(1, 1).wait_recv()

    @pl.when(jnp.logical_not(has_dn))
    def _():
        halo[:, 1] = jnp.zeros((2, EDGE, cols), F32)

    def around_edges(which):
        ref = (surf, kap)[which]
        return jnp.concatenate(
            [halo[which, 0], ref[0, 0:EDGE, :], ref[0, rows - EDGE : rows, :], halo[which, 1]], axis=0
        )

    edges = diffuse(around_edges(0), around_edges(1))
    top, bottom = edges[EDGE : 2 * EDGE], edges[2 * EDGE : 3 * EDGE]
    upper = lax.broadcasted_iota(jnp.int32, (EDGE, cols), 0) < SUBSTEPS
    edge = jnp.where(upper, top, bottom)
    out[0, 0:SUBSTEPS, :] = edge[0:SUBSTEPS]
    out[0, rows - SUBSTEPS : rows, :] = edge[SUBSTEPS:EDGE]
    blk[n_inner:n_blk, :] = columns_of(edge, width).astype(BF16)

    @pl.loop(0, n_oth)
    def _(j):
        block_copy(j, mine, True).start()

    ids = block_ids((n_blk, cap), rows, per_row)
    slot_of = lax.broadcasted_iota(jnp.int32, (n_k * n_t, cap), 1)

    @pl.loop(0, n_oth)
    def _(j):
        sl_copy(j, j).wait_recv()
        sent = sl_in[j, pl.ds(lax.rem(me_s, 8), 1), :]
        pick = jnp.where(ids == sent, 1.0, 0.0).astype(BF16)
        wanted = jnp.concatenate([asked[...]] * pl.cdiv(cap, width), axis=1)[:, :cap]
        slots = (slot_of + (oth_base + j) * cap).astype(F32)
        put = jnp.where(wanted == slots, 1.0, 0.0).astype(BF16)
        chosen = lax.dot_general(put, pick, (((1,), (1,)), ((), ())), preferred_element_type=F32)
        cmat[j] = chosen.astype(BF16)

    acc[...] = jnp.zeros_like(acc)

    @pl.loop(0, n_oth)
    def _(j):
        block_copy(j, j, False).wait_recv()
        block_copy(j, j, True).wait_recv()
        acc[...] += jnp.dot(cmat[j], land[j], preferred_element_type=F32)

    for k in range(n_k):
        gbf[k] = acc[k * n_t : (k + 1) * n_t, :].astype(BF16)

    def pair_copy(i, slot):
        to = lax.rem(me_f + i, n_fld)
        return pltpu.make_async_remote_copy(
            src_ref=gbf.at[:, pl.ds(pl.multiple_of(to * t_loc, t_loc), t_loc), :],
            dst_ref=gath.at[slot],
            send_sem=g_send.at[i],
            recv_sem=g_recv.at[i],
            device_id={"sec": me_s, "fld": to},
            device_id_type=MESH,
        )

    for i in range(1, n_fld):
        pair_copy(i, me_f).start()
    gath[me_f] = gbf[:, pl.ds(pl.multiple_of(me_f * t_loc, t_loc), t_loc), :]
    loads[4].wait()
    for i in range(1, n_fld):
        pair_copy(i, lax.rem(me_f + n_fld - i, n_fld)).wait_recv()

    for f in range(n_fld):
        for k in range(n_k):
            xs[k, pl.ds(f, t_loc, stride=n_fld), :] = gath[f, k].astype(F32)

    group = 8 // n_fld
    which_t = lax.broadcasted_iota(jnp.int32, (8, width), 0) // n_fld

    def remap(g, carry):
        at = pl.multiple_of(g * 8, 8)
        x = jnp.concatenate([xs[k, pl.ds(at, 8), :] for k in range(n_k)], axis=1).astype(BF16)
        y = jnp.zeros((8, width), F32)
        for u in range(group):
            w = jnp.concatenate([wv[g * group + u, k] for k in range(n_k)], axis=1)
            full = lax.dot_general(x, w, (((1,), (1,)), ((), ())), preferred_element_type=F32)
            y = jnp.where(which_t == u, full, y)
        ys[pl.ds(at, 8), :] = y
        return carry

    lax.fori_loop(0, t_loc // group, remap, 0, unroll=16)

    for f in range(n_fld):
        ret[f] = ys[pl.ds(f, t_loc, stride=n_fld), :].astype(BF16)

    def return_copy(i, slot):
        to = lax.rem(me_f + i, n_fld)
        return pltpu.make_async_remote_copy(
            src_ref=ret.at[to],
            dst_ref=back.at[slot],
            send_sem=r_send.at[i],
            recv_sem=r_recv.at[i],
            device_id={"sec": me_s, "fld": to},
            device_id_type=MESH,
        )

    for i in range(1, n_fld):
        return_copy(i, me_f).start()
    back[me_f] = ret[me_f]
    for i in range(1, n_fld):
        return_copy(i, lax.rem(me_f + n_fld - i, n_fld)).wait_recv()
    for q in range(n_fld):
        res[q * t_loc : (q + 1) * t_loc, :] = back[q].astype(F32)
    for c in range(per_row):
        out[1, :, c * width : (c + 1) * width] = res[pl.ds(c, rows, stride=per_row), :]

    @pl.when(has_dn)
    def _():
        halo_copy(0, 0).wait_send()
        halo_copy(1, 0).wait_send()

    @pl.when(has_up)
    def _():
        halo_copy(0, 1).wait_send()
        halo_copy(1, 1).wait_send()

    @pl.loop(0, n_oth)
    def _(j):
        sl_copy(j, mine).wait_send()
        block_copy(j, mine, False).wait_send()
        block_copy(j, mine, True).wait_send()

    for i in range(1, n_fld):
        pair_copy(i, me_f).wait_send()
        return_copy(i, me_f).wait_send()


def per_device(n_sec, n_fld, surface, diffusivity, send_list, recv_slot, weights):
    _, rows, cols = surface.shape
    t_loc, n_k, width, _ = weights.shape
    n_t = recv_slot.shape[0]
    n_blk = rows * cols // width
    cap = send_list.shape[2]
    most = n_sec - n_sec * 3 // 8
    vmem = pl.BlockSpec(memory_space=pltpu.VMEM)
    dma = pltpu.SemaphoreType.DMA
    operands = [pltpu.with_memory_space_constraint(x, pltpu.HBM) for x in (surface, diffusivity, send_list, recv_slot.T, weights)]
    both = pl.pallas_call(
        functools.partial(kernel, n_sec, n_fld),
        out_shape=pltpu.VMEM((2, rows, cols), F32),
        in_specs=[pl.BlockSpec(memory_space=pltpu.HBM)] * 5,
        out_specs=vmem,
        scratch_shapes=[
            pltpu.VMEM(surface.shape, F32),
            pltpu.VMEM(surface.shape, F32),
            pltpu.VMEM(send_list.shape, jnp.int32),
            pltpu.VMEM((n_k, n_t), jnp.int32),
            pltpu.VMEM((2, 2, EDGE, cols), F32),
            pltpu.VMEM(weights.shape, BF16),
            pltpu.VMEM((most, 8, cap), jnp.int32),
            pltpu.VMEM((n_blk, width), BF16),
            pltpu.VMEM((most, n_blk, width), BF16),
            pltpu.VMEM((most, n_k * n_t, n_blk), BF16),
            pltpu.VMEM((n_k * n_t, width), F32),
            pltpu.VMEM((n_k * n_t, width), F32),
            pltpu.VMEM((n_k, n_t, width), BF16),
            pltpu.VMEM((n_fld, n_k, t_loc, width), BF16),
            pltpu.VMEM((n_k, t_loc * n_fld, width), F32),
            pltpu.VMEM((t_loc * n_fld, width), F32),
            pltpu.VMEM((n_fld, t_loc, width), BF16),
            pltpu.VMEM((n_fld, t_loc, width), BF16),
            pltpu.VMEM((n_blk, width), F32),
            dma((5,)),
            dma((2, 2)),
            dma((2, 2)),
            dma((most,)),
            dma((most,)),
            dma((most,)),
            dma((most,)),
            dma((most,)),
            dma((most,)),
            dma((n_fld,)),
            dma((n_fld,)),
            dma((n_fld,)),
            dma((n_fld,)),
        ],
        compiler_params=pltpu.CompilerParams(
            collective_id=0, has_side_effects=True, vmem_limit_bytes=48 * 1024 * 1024
        ),
    )(*operands)
    return both[0:1], both[1:2]


def solution(mesh):
    return jax.shard_map(
        functools.partial(per_device, mesh.shape["sec"], mesh.shape["fld"]),
        mesh=mesh,
        in_specs=(
            P("fld", "sec", None),
            P("fld", "sec", None),
            P("sec", None, None),
            P("sec", None),
            P(("sec", "fld"), None, None, None),
        ),
        out_specs=(P("fld", "sec", None), P("fld", "sec", None)),
        check_vma=False,
    )
```
